32 devices in a mesh: rows: 8 (over z, y), snaps: 4 (over x, core).
Axes of the slice: x: 2, y: 2, z: 4, core: 2. Of those that a mesh axis runs over, the one named last changes fastest.
Arguments:
- stress: float32 [131072, 1024], P('rows', 'snaps'), may hold values from -80 to 80
- sketch: float32 [64, 1024], P(None, 'snaps'), may hold values from -0.1875 to 0.1875
Outputs:
- basis: float32 [64, 131072], P(None, ('rows', 'snaps'))
- coeffs: float32 [64, 1024], P(None, 'snaps')
- spectrum: float32 [64, 64], replicated
The draws below stay inside these ranges and needn't reach their ends.
All inputs are finite; a program needn't handle non-finite values.
Results may differ from the reference program's by a relative error of at most 0.0015.
Values sent between devices are 32-bit elements; how exact they have to be, the bound alone decides.
A program may use at most 128 MiB of HBM per device.

```python
import math
import jax
import jax.numpy as jnp
from jax import lax

K = 64
SNAPS = 1024
TOTAL_ROWS = 131072


def draw_stress(key, part):
    streams = jax.random.split(key, 4)
    mode_count = 2 * K
    fall_rate = math.log(12.0) / K
    strength_norm = math.sqrt(sum((math.exp(-2.0 * fall_rate * index) for index in range(mode_count))))
    mode_weights = jnp.exp(-fall_rate * jnp.arange(mode_count, dtype=jnp.float32)) / strength_norm
    noise_level = math.sqrt(SNAPS) / (25.0 * strength_norm)
    left_factor = jnp.clip(jax.random.normal(streams[0], (TOTAL_ROWS, mode_count), jnp.float32), -4.0, 4.0)
    right_factor = jnp.clip(jax.random.normal(streams[1], (mode_count, SNAPS), jnp.float32), -4.0, 4.0)
    background = jnp.clip(jax.random.normal(streams[2], (TOTAL_ROWS, SNAPS), jnp.float32), -4.0, 4.0)
    jitter = jnp.ones((TOTAL_ROWS, 1), jnp.float32)
    log_three = 1.0986123
    row_place = jnp.arange(TOTAL_ROWS, dtype=jnp.float32) / TOTAL_ROWS
    column_place = jnp.arange(SNAPS, dtype=jnp.float32) / SNAPS
    row_factor = jnp.exp(log_three * row_place)[:, None] * jitter
    column_factor = jnp.exp(log_three * column_place)[None, :]
    modal_part = jnp.dot(left_factor * mode_weights[None, :], right_factor, precision=lax.Precision.HIGHEST)
    values = (modal_part + noise_level * background) * row_factor * column_factor / 3.0
    return jnp.clip(values, -80.0, 80.0).astype(jnp.float32)


def block_scale(stream_key, shape, pieces, smallest, high):
    level = 1.0
    for position, parts in pieces:
        draws = jax.random.uniform(jax.random.fold_in(jax.random.fold_in(stream_key, 6), position), (parts,), jnp.float32, smallest / len(pieces), high / len(pieces))
        level = level * jnp.repeat(jnp.exp(draws), shape[position] // parts).reshape((-1,) + (1,) * (len(shape) - 1 - position))
    return level


def scatter_about(own_key, dims, width, limit, cuts=(), held_as=jnp.bfloat16):
    result = jax.random.normal(own_key, dims, jnp.float32) * width
    if len(cuts) > 0:
        result = block_scale(own_key, dims, cuts, -0.22, 0.18) * result
    return jnp.clip(result, min=-limit, max=limit).astype(held_as)


def setup_inputs(seed: int = 0) -> dict:
    splits = jax.random.split(jax.random.key(seed), 3)
    return {
        "stress": draw_stress(jax.random.fold_in(splits[2], 71), 0),
        "sketch": scatter_about(splits[1], (K, SNAPS), SNAPS ** -0.5, 0.1875, ((1, 4),), jnp.float32),
    }


def product(left_m, right_m, left_dim, right_dim):
    return lax.dot_general(left_m.astype(jnp.float32), right_m.astype(jnp.float32), (((left_dim,), (right_dim,)), ((), ())), precision=lax.Precision.HIGHEST, preferred_element_type=jnp.float32)

def inverse_factor(gram_total):
    lower = jnp.linalg.cholesky(gram_total)
    ident = jnp.eye(gram_total.shape[0], dtype=gram_total.dtype)
    return lax.linalg.triangular_solve(lower, ident, left_side=True, lower=True)

def orthonormal(panel):
    factor = inverse_factor(product(panel, panel, 1, 1))
    return product(factor, panel, 1, 0)

def reference(stress, sketch):
    operand = sketch
    basis = None
    for turn in range(2):
        panel = product(operand, stress, 1, 1)
        basis = orthonormal(panel)
        operand = product(basis, stress, 1, 0)
    scale = jnp.sqrt(jnp.float32(TOTAL_ROWS))
    spectrum = product(operand, operand, 1, 1) / SNAPS
    return (basis * scale, operand, spectrum)
```

```python
import functools
import math

import jax
import jax.numpy as jnp
from jax import lax
from jax.experimental import pallas as pl
from jax.experimental.pallas import tpu as pltpu
from jax.sharding import PartitionSpec as P

MESH = pl.DeviceIdType.MESH
F32 = jnp.float32
BF16 = jnp.bfloat16
CHUNK = 1024
HALF = CHUNK // 2
SLOTS = 4
PIECE = 128
PHASES = 4
LEAD = 5
EARLY = 3
LATE = 6


def dot(left_m, right_m, left_dim, right_dim, precision=None):
    return lax.dot_general(
        left_m,
        right_m,
        (((left_dim,), (right_dim,)), ((), ())),
        precision=precision,
        preferred_element_type=F32,
    )


def dot_full(left_m, right_m, left_dim, right_dim):
    return dot(left_m, right_m, left_dim, right_dim, lax.Precision.HIGHEST)


def split(value):
    high = value.astype(BF16)
    low = (value - high.astype(F32)).astype(BF16)
    return high, low


def inverse_factor(gram):
    k = gram.shape[0]
    line = lax.broadcasted_iota(jnp.int32, (k, k), 0)
    lane = lax.broadcasted_iota(jnp.int32, (k, k), 1)
    wide_line = lax.broadcasted_iota(jnp.int32, (k, 2 * k), 0)
    ident = jnp.where(line == lane, 1.0, 0.0).astype(F32)
    table = jnp.concatenate([gram, ident], axis=1)
    for j in range(k - 1):
        row = table[j : j + 1, :]
        row = row / row[:, j : j + 1]
        column = jnp.where(wide_line > j, table[:, j : j + 1], 0.0)
        table = table - column * row
    diag = jnp.sum(jnp.where(line == lane, table[:, :k], 0.0), axis=1, keepdims=True)
    return table[:, k:] / jnp.sqrt(diag)


def solve_first(zone, width):
    h = zone.shape[0]
    f11 = inverse_factor(zone[:, width : width + h])
    return f11, dot_full(f11, zone[:, 0:width], 1, 0)


def solve_second(gram, f11):
    h = f11.shape[0]
    l21 = dot_full(gram[:, 0:h], f11, 1, 1)
    f22 = inverse_factor(gram[:, h : 2 * h] - dot_full(l21, l21, 1, 1))
    f21 = -dot_full(f22, dot_full(l21, f11, 1, 0), 1, 0)
    return f21, f22


def kernel(
    ranks, batch_total,
    stress, sketch, share_out, factor_out, coeffs_out, spectrum_out,
    stage, high, low, operand, later, part, got1, summed, got2, panel,
    acc, spread, landed, total, full, zone, first, spect, gram, grams, lead_factor,
    stage_sem, share_sem, send1, recv1, send2, recv2, send3, recv3,
    rs_send, rs_recv, ag_send, ag_recv, sp_send, sp_recv, gr_send, gr_recv,
):
    groups = 4
    k = sketch.shape[0]
    kp = k // 2
    width = stress.shape[1]
    chunks = summed.shape[0]
    lines = kp // ranks
    me_row = lax.axis_index("rows")
    me = lax.axis_index("snaps")
    mine = me % 2
    core = me + 1 - 2 * mine
    chip = (me + 2) % groups
    units = PHASES * chunks

    def load(c):
        slot = c % SLOTS
        return pltpu.make_async_copy(
            stress.at[pl.ds(c * CHUNK, CHUNK), :], stage.at[slot], stage_sem.at[slot]
        )

    for c in range(SLOTS):
        load(c).start()

    barrier = pltpu.get_barrier_semaphore()
    for d in range(1, ranks):
        pl.semaphore_signal(
            barrier, inc=1, device_id={"rows": (me_row + d) % ranks}, device_id_type=MESH
        )
    for d in range(1, groups):
        pl.semaphore_signal(
            barrier, inc=1, device_id={"snaps": (me + d) % groups}, device_id_type=MESH
        )

    def remote(src, dst, s_sem, r_sem, device):
        return pltpu.make_async_remote_copy(
            src_ref=src, dst_ref=dst, send_sem=s_sem, recv_sem=r_sem,
            device_id=device, device_id_type=MESH,
        )

    def hop1(p, c):
        return remote(
            part.at[p % 2, c, 1 - mine], got1.at[p, c], send1.at[p, c], recv1.at[p, c],
            {"snaps": core},
        )

    def hop2(p, c):
        return remote(summed.at[c], got2.at[p, c], send2.at[p, c], recv2.at[p, c], {"snaps": chip})

    def hop3(p, c):
        return remote(
            panel.at[p, c, mine], panel.at[p, c, mine], send3.at[p, c], recv3.at[p, c],
            {"snaps": core},
        )

    def scatter(p, d):
        to = (me_row + d) % ranks
        return remote(
            spread.at[p, to], landed.at[p, d], rs_send.at[p, d], rs_recv.at[p, d], {"rows": to}
        )

    def gather(p, d):
        to = (me_row + d) % ranks
        return remote(
            total.at[p], full.at[p, me_row], ag_send.at[p, d], ag_recv.at[p, d], {"rows": to}
        )

    def give_gram(d):
        return remote(
            gram, grams.at[me_row], gr_send.at[d], gr_recv.at[d], {"rows": (me_row + d) % ranks}
        )

    def share_spectrum(d):
        return remote(
            spect.at[0], spect.at[d], sp_send.at[d], sp_recv.at[d], {"snaps": (me + d) % groups}
        )

    def share_copy(i):
        per = chunks // groups
        return pltpu.make_async_copy(
            panel.at[2 + i, pl.ds(me * per, per)],
            share_out.at[i],
            share_sem.at[i],
        )

    def convert(c):
        slot = c % SLOTS
        load(c).wait()

        def body(p, carry):
            h, l = split(stage[slot, pl.ds(p * PIECE, PIECE), :])
            at = pl.ds(c * CHUNK + p * PIECE, PIECE)
            high[at, :] = h
            low[at, :] = l
            return carry

        lax.fori_loop(0, CHUNK // PIECE, body, 0)

        @pl.when(c + SLOTS < chunks)
        def _():
            load(c + SLOTS).start()

    def produce(p, c):
        @pl.when(p == 0)
        def _():
            convert(c)
            for h in range(2):
                at = pl.ds(c * CHUNK + h * HALF, HALF)
                both = dot(operand[...], high[at, :], 1, 1)
                rest = dot(operand[0:k, :], low[at, :], 1, 1)
                value = both[0:k] + (both[k : 2 * k] + rest)
                part[0, c, h] = value[0:kp]
                part[1, c, h] = value[kp:k]

        @pl.when(p >= 2)
        def _():
            i = p % 2
            for h in range(2):
                at = pl.ds(c * CHUNK + h * HALF, HALF)
                both = dot(later[i], high[at, :], 1, 1)
                rest = dot(later[i, 0:kp, :], low[at, :], 1, 1)
                part[i, c, h] = both[0:kp] + (both[kp:k] + rest)

        hop1(p, c).start()

    def add_cores(p, c):
        hop1(p, c).wait()
        summed[c] = part[p % 2, c, mine] + got1[p, c]
        hop2(p, c).start()

    def add_chips(p, c):
        hop2(p, c).wait()
        panel[p, c, mine] = summed[c] + got2[p, c]
        hop3(p, c).start()

    def accumulate(p, c):
        hop3(p, c).wait()
        for h in range(2):
            value = panel[p, c, h]
            hi, lo = split(value)
            at = pl.ds(c * CHUNK + h * HALF, HALF)
            both = dot(jnp.concatenate([hi, lo], axis=0), high[at, :], 1, 0)
            rest = dot(hi, low[at, :], 1, 0)
            acc[:, 0:width] += both[0:kp] + (both[kp:k] + rest)

        @pl.when(p % 2 == 0)
        def _():
            for h in range(2):
                value = panel[p, c, h]
                acc[:, width : width + kp] += dot_full(value, value, 1, 1)

        @pl.when(p % 2 == 1)
        def _():
            for h in range(2):
                value = panel[p, c, h]
                pair = jnp.concatenate([panel[p - 1, c, h], value], axis=0)
                acc[:, width : width + k] += dot_full(value, pair, 1, 1)

    def reduce_start(p):
        for r in range(ranks):
            spread[p, r] = acc[r * lines : (r + 1) * lines, :]
        acc[...] = jnp.zeros_like(acc)
        for d in range(1, ranks):
            scatter(p, d).start()

    def reduce_share(p):
        value = spread[p, me_row]
        for d in range(1, ranks):
            scatter(p, d).wait()
            value = value + landed[p, d]
        total[p] = value
        full[p, me_row] = value
        for d in range(1, ranks):
            gather(p, d).start()

    def reduce_end(p):
        for d in range(1, ranks):
            gather(p, d).wait()
        for r in range(ranks):
            zone[r * lines : (r + 1) * lines, :] = full[p, r]

    def set_later(i, value):
        h, l = split(value)
        later[i, 0:kp, :] = h
        later[i, kp:k, :] = l

    h, l = split(sketch[...])
    operand[0:k, :] = h
    operand[k : 2 * k, :] = l
    acc[...] = jnp.zeros_like(acc)
    pl.semaphore_wait(barrier, ranks - 1 + groups - 1)
    wait1, wait2 = EARLY * chunks // 16, LATE * chunks // 16

    def step(s, carry):
        @pl.when(s < units)
        def _():
            produce(s // chunks, s % chunks)

        @pl.when(jnp.logical_and(s >= 1, s <= units))
        def _():
            u = s - 1
            add_cores(u // chunks, u % chunks)

        @pl.when(jnp.logical_and(s >= 1 + LEAD, s <= units + LEAD))
        def _():
            u = s - 1 - LEAD
            add_chips(u // chunks, u % chunks)

        @pl.when(s >= 2 + LEAD)
        def _():
            u = s - 2 - LEAD
            accumulate(u // chunks, u % chunks)

        since = s - (chunks + LEAD + 1)
        done = since // chunks
        at = since % chunks
        live = jnp.logical_and(since >= 0, done < PHASES - 1)

        @pl.when(jnp.logical_and(live, at == 0))
        def _():
            reduce_start(done)

        @pl.when(jnp.logical_and(live, at == wait1))
        def _():
            reduce_share(done)

        @pl.when(jnp.logical_and(live, at == wait2))
        def _():
            reduce_end(done)

            @pl.when(done % 2 == 0)
            def _():
                f11, value = solve_first(zone[...], width)
                lead_factor[...] = f11
                first[0] = zone[:, 0:width]
                first[1] = value
                set_later(0, value)

            @pl.when(done % 2 == 1)
            def _():
                f21, f22 = solve_second(zone[:, width : width + k], lead_factor[...])
                value = dot_full(f21, first[0], 1, 0) + dot_full(f22, zone[:, 0:width], 1, 0)
                set_later(1, value)

        return carry

    lax.fori_loop(0, units + LEAD + 2, step, 0)

    own_gram = acc[:, width : width + k]
    gram[...] = own_gram
    grams[me_row] = own_gram
    for d in range(1, ranks):
        give_gram(d).start()
    reduce_start(3)
    for i in range(2):
        share_copy(i).start()
    for d in range(1, ranks):
        give_gram(d).wait_recv()
    gram_total = grams[0]
    for r in range(1, ranks):
        gram_total = gram_total + grams[r]
    reduce_share(3)
    f21, f22 = solve_second(gram_total, lead_factor[...])
    factor_out[0:kp, :] = jnp.concatenate([lead_factor[...], jnp.zeros((kp, kp), F32)], axis=1)
    factor_out[kp:k, :] = jnp.concatenate([f21, f22], axis=1)
    reduce_end(3)
    coeffs_out[0:kp, :] = first[1]
    coeffs_out[kp:k, :] = dot_full(f21, first[0], 1, 0) + dot_full(f22, zone[:, 0:width], 1, 0)
    sums = coeffs_out[...]
    spect[0] = dot_full(sums, sums, 1, 1)
    for d in range(1, groups):
        share_spectrum(d).start()
    for d in range(1, ranks):
        give_gram(d).wait_send()
    for i in range(2):
        share_copy(i).wait()
    for d in range(1, groups):
        share_spectrum(d).wait()
    a = spect[0] + spect[2]
    b = spect[1] + spect[3]
    spectrum_out[...] = (a + b) / batch_total


def finish(scale, factor, share, coeffs, spectrum, basis_out, coeffs_out, spectrum_out):
    scaled = factor[...] * scale
    for h in range(2):
        both = jnp.concatenate([share[0, 0, h], share[1, 0, h]], axis=0)
        basis_out[:, h * HALF : (h + 1) * HALF] = dot_full(scaled, both, 1, 0)
    coeffs_out[...] = coeffs[...]
    spectrum_out[...] = spectrum[...]


def on_device(stress, sketch):
    rows_dev, width = stress.shape
    k = sketch.shape[0]
    kp = k // 2
    groups = lax.axis_size("snaps")
    ranks = lax.axis_size("rows")
    share = rows_dev // groups
    chunks = rows_dev // CHUNK
    lines = kp // ranks
    wide = width + 128
    scale = math.sqrt(float(rows_dev * ranks))
    vmem = pl.BlockSpec(memory_space=pltpu.VMEM)
    dma = pltpu.SemaphoreType.DMA
    per = chunks // groups
    part_out, factor, coeffs, spectrum = pl.pallas_call(
        functools.partial(kernel, ranks, float(width * groups)),
        out_shape=(
            jax.ShapeDtypeStruct((2, per, 2, kp, HALF), F32),
            jax.ShapeDtypeStruct((k, k), F32),
            jax.ShapeDtypeStruct((k, width), F32),
            jax.ShapeDtypeStruct((k, k), F32),
        ),
        in_specs=[pl.BlockSpec(memory_space=pl.ANY), vmem],
        out_specs=(pl.BlockSpec(memory_space=pl.ANY), vmem, vmem, vmem),
        scratch_shapes=[
            pltpu.VMEM((SLOTS, CHUNK, width), F32),
            pltpu.VMEM((rows_dev, width), BF16),
            pltpu.VMEM((rows_dev, width), BF16),
            pltpu.VMEM((2 * k, width), BF16),
            pltpu.VMEM((2, k, width), BF16),
            pltpu.VMEM((2, chunks, 2, kp, HALF), F32),
            pltpu.VMEM((PHASES, chunks, kp, HALF), F32),
            pltpu.VMEM((chunks, kp, HALF), F32),
            pltpu.VMEM((PHASES, chunks, kp, HALF), F32),
            pltpu.VMEM((PHASES, chunks, 2, kp, HALF), F32),
            pltpu.VMEM((kp, wide), F32),
            pltpu.VMEM((PHASES, ranks, lines, wide), F32),
            pltpu.VMEM((PHASES, ranks, lines, wide), F32),
            pltpu.VMEM((PHASES, lines, wide), F32),
            pltpu.VMEM((PHASES, ranks, lines, wide), F32),
            pltpu.VMEM((kp, wide), F32),
            pltpu.VMEM((2, kp, width), F32),
            pltpu.VMEM((groups, k, k), F32),
            pltpu.VMEM((kp, k), F32),
            pltpu.VMEM((ranks, kp, k), F32),
            pltpu.VMEM((kp, kp), F32),
            dma((SLOTS,)),
            dma((2,)),
            dma((PHASES, chunks)),
            dma((PHASES, chunks)),
            dma((PHASES, chunks)),
            dma((PHASES, chunks)),
            dma((PHASES, chunks)),
            dma((PHASES, chunks)),
            dma((PHASES, ranks)),
            dma((PHASES, ranks)),
            dma((PHASES, ranks)),
            dma((PHASES, ranks)),
            dma((groups,)),
            dma((groups,)),
            dma((ranks,)),
            dma((ranks,)),
        ],
        compiler_params=pltpu.CompilerParams(
            collective_id=0, has_side_effects=True, vmem_limit_bytes=58 * 1024 * 1024
        ),
        cost_estimate=pl.CostEstimate(
            flops=24 * rows_dev * width * k, bytes_accessed=rows_dev * width * 4, transcendentals=0
        ),
    )(stress, sketch)
    same = lambda i: (0, 0)
    return pl.pallas_call(
        functools.partial(finish, scale),
        grid=(per,),
        out_shape=(
            jax.ShapeDtypeStruct((k, share), F32),
            jax.ShapeDtypeStruct((k, width), F32),
            jax.ShapeDtypeStruct((k, k), F32),
        ),
        in_specs=[
            pl.BlockSpec((k, k), same),
            pl.BlockSpec((2, 1, 2, kp, HALF), lambda i: (0, i, 0, 0, 0)),
            pl.BlockSpec((k, width), same),
            pl.BlockSpec((k, k), same),
        ],
        out_specs=(
            pl.BlockSpec((k, CHUNK), lambda i: (0, i)),
            pl.BlockSpec((k, width), same),
            pl.BlockSpec((k, k), same),
        ),
    )(factor, part_out, coeffs, spectrum)


def solution(mesh):
    placed = (P("rows", "snaps"), P(None, "snaps"))
    return jax.shard_map(
        on_device,
        mesh=mesh,
        in_specs=placed,
        out_specs=(P(None, ("rows", "snaps")), P(None, "snaps"), P()),
        check_vma=False,
    )
```

```python
import functools
import math

import jax
import jax.numpy as jnp
from jax import lax
from jax.experimental import pallas as pl
from jax.experimental.pallas import tpu as pltpu
from jax.sharding import PartitionSpec as P

MESH = pl.DeviceIdType.MESH
F32 = jnp.float32
BF16 = jnp.bfloat16
CHUNK = 2048
HALF = CHUNK // 2
SLOTS = 2
PIECE = 128
CUTS = 4
PIECES = 4
PHASES = 4
LEAD = 3
EARLY = 3
LATE = 6
PAIR = 1
BACK = 1


def dot(left_m, right_m, left_dim, right_dim, precision=None):
    return lax.dot_general(
        left_m,
        right_m,
        (((left_dim,), (right_dim,)), ((), ())),
        precision=precision,
        preferred_element_type=F32,
    )


def dot_full(left_m, right_m, left_dim, right_dim):
    return dot(left_m, right_m, left_dim, right_dim, lax.Precision.HIGHEST)


def split(value):
    high = value.astype(BF16)
    low = (value - high.astype(F32)).astype(BF16)
    return high, low


def inverse_factor(gram):
    k = gram.shape[0]
    line = lax.broadcasted_iota(jnp.int32, (k, k), 0)
    lane = lax.broadcasted_iota(jnp.int32, (k, k), 1)
    wide_line = lax.broadcasted_iota(jnp.int32, (k, 2 * k), 0)
    ident = jnp.where(line == lane, 1.0, 0.0).astype(F32)
    table = jnp.concatenate([gram, ident], axis=1)
    for j in range(k - 1):
        row = table[j : j + 1, :]
        row = row / row[:, j : j + 1]
        column = jnp.where(wide_line > j, table[:, j : j + 1], 0.0)
        table = table - column * row
    diag = jnp.sum(jnp.where(line == lane, table[:, :k], 0.0), axis=1, keepdims=True)
    return table[:, k:] / jnp.sqrt(diag)


def below(gram, f11):
    h = f11.shape[0]
    l21 = dot_full(gram[:, 0:h], f11, 1, 1)
    return l21, gram[:, h : 2 * h] - dot_full(l21, l21, 1, 1)


def kernel(
    ranks, batch_total, scale,
    stress, sketch, basis_out, coeffs_out, spectrum_out,
    stage, high, low, operand, part, got1, summed, got2, panel,
    acc, gacc, spread, landed, total, full, zone, lead, basis, spect, gram, grams, lead_factor,
    stage_sem, basis_sem, send1, recv1, send2, recv2, send3, recv3,
    rs_send, rs_recv, ag_send, ag_recv, sp_send, sp_recv, gr_send, gr_recv,
):
    groups = 4
    k = sketch.shape[0]
    kp = k // 2
    width = stress.shape[1]
    chunks = summed.shape[0]
    lines = kp // ranks
    me_row = lax.axis_index("rows")
    me = lax.axis_index("snaps")
    mine = me % 2
    core = me + 1 - 2 * mine
    chip = (me + 2) % groups
    units = PHASES * chunks
    per = chunks // groups
    blocks = [(i, h, (2 * i + h) * HALF) for i in range(per) for h in range(2)]

    def load(c, q):
        slot = c % SLOTS
        rows = CHUNK // CUTS
        return pltpu.make_async_copy(
            stress.at[pl.ds(c * CHUNK + q * rows, rows), :],
            stage.at[slot, pl.ds(q * rows, rows), :],
            stage_sem.at[slot, q],
        )

    for q in range(CUTS):
        load(0, q).start()

    barrier = pltpu.get_barrier_semaphore()
    for d in range(1, ranks):
        pl.semaphore_signal(
            barrier, inc=1, device_id={"rows": (me_row + d) % ranks}, device_id_type=MESH
        )
    for d in range(1, groups):
        pl.semaphore_signal(
            barrier, inc=1, device_id={"snaps": (me + d) % groups}, device_id_type=MESH
        )

    def remote(src, dst, s_sem, r_sem, device):
        return pltpu.make_async_remote_copy(
            src_ref=src, dst_ref=dst, send_sem=s_sem, recv_sem=r_sem,
            device_id=device, device_id_type=MESH,
        )

    def hop1(p, c):
        return remote(
            part.at[c, 1 - mine], got1.at[p, c], send1.at[p, c], recv1.at[p, c],
            {"snaps": core},
        )

    def hop2(p, c):
        return remote(summed.at[c], got2.at[p, c], send2.at[p, c], recv2.at[p, c], {"snaps": chip})

    def hop3(p, c):
        return remote(
            panel.at[p, c, mine], panel.at[p, c, mine], send3.at[p, c], recv3.at[p, c],
            {"snaps": core},
        )

    def scatter(p, d, lanes=None):
        to = (me_row + d) % ranks
        src, dst = spread.at[p, to], landed.at[p, d]
        if lanes is not None:
            src, dst = src.at[:, 0:lanes], dst.at[:, 0:lanes]
        return remote(src, dst, rs_send.at[p, d], rs_recv.at[p, d], {"rows": to})

    def gather(p, d, lanes=None):
        to = (me_row + d) % ranks
        src, dst = total.at[p], full.at[p, me_row]
        if lanes is not None:
            src, dst = src.at[:, 0:lanes], dst.at[:, 0:lanes]
        return remote(src, dst, ag_send.at[p, d], ag_recv.at[p, d], {"rows": to})

    def give_gram(d):
        return remote(
            gram, grams.at[me_row], gr_send.at[d], gr_recv.at[d], {"rows": (me_row + d) % ranks}
        )

    def share_spectrum(d):
        return remote(
            spect.at[0], spect.at[d], sp_send.at[d], sp_recv.at[d], {"snaps": (me + d) % groups}
        )

    def basis_copy(i):
        at = pl.ds(i * kp, kp)
        return pltpu.make_async_copy(basis.at[at, :], basis_out.at[at, :], basis_sem.at[i])

    def convert(c):
        slot = c % SLOTS

        @pl.when(c + 1 < chunks)
        def _():
            for q in range(CUTS):
                load(c + 1, q).start()

        per_cut = CHUNK // CUTS // PIECE
        for q in range(CUTS):
            load(c, q).wait()

            def body(i, carry):
                h, l = split(stage[slot, pl.ds(i * PIECE, PIECE), :])
                at = pl.ds(c * CHUNK + i * PIECE, PIECE)
                high[at, :] = h
                low[at, :] = l
                return carry

            lax.fori_loop(q * per_cut, (q + 1) * per_cut, body, 0)

    def project(p, c, h):
        at = pl.ds(c * CHUNK + h * HALF, HALF)
        both = dot(operand[p], high[at, :], 1, 1)
        rest = dot(operand[p, 0:kp, :], low[at, :], 1, 1)
        part[c, h] = both[0:kp] + (both[kp:k] + rest)

    def produce(p, c):
        @pl.when(p == 0)
        def _():
            convert(c)

        project(p, c, 1 - mine)

        @pl.when(jnp.logical_and(p == 0, c == 0))
        def _():
            pl.semaphore_wait(barrier, ranks - 1 + groups - 1)

        hop1(p, c).start()
        project(p, c, mine)

    def add_cores(p, c):
        hop1(p, c).wait()
        summed[c] = part[c, mine] + got1[p, c]
        hop2(p, c).start()

    def add_chips(p, c):
        hop2(p, c).wait()
        panel[p, c, mine] = summed[c] + got2[p, c]
        hop3(p, c).start()

    def stacked(p, c):
        value = jnp.concatenate([panel[p, c, 0], panel[p, c, 1]], axis=1)
        hi, lo = split(value)
        return jnp.concatenate([hi, lo], axis=0)

    def accumulate(p, c):
        hop3(p, c).wait()
        stack = stacked(p, c)
        at = pl.ds(c * CHUNK, CHUNK)
        both = dot(stack, high[at, :], 1, 0)
        rest = dot(stack[0:kp], low[at, :], 1, 0)
        acc[:, 0:width] += both[0:kp] + (both[kp:k] + rest)

        @pl.when(p % 2 == 0)
        def _():
            gacc[:, 0:k] += dot(stack, stack, 1, 1)

        @pl.when(p % 2 == 1)
        def _():
            gacc[...] += dot(stack, jnp.concatenate([stacked(p - 1, c), stack], axis=0), 1, 1)

    def fold_gram():
        rows = gacc[0:kp, :] + gacc[kp:k, :]
        for i in range(2):
            at = i * k
            acc[:, width + i * kp : width + (i + 1) * kp] = (
                rows[:, at : at + kp] + rows[:, at + kp : at + k]
            )
        gacc[...] = jnp.zeros_like(gacc)

    def reduce_start(p, lanes=None):
        for r in range(ranks):
            spread[p, r] = acc[r * lines : (r + 1) * lines, :]
        acc[...] = jnp.zeros_like(acc)
        for d in range(1, ranks):
            scatter(p, d, lanes).start()

    def reduce_share(p, lanes=None):
        value = spread[p, me_row]
        for d in range(1, ranks):
            scatter(p, d, lanes).wait()
            value = value + landed[p, d]
        total[p] = value
        full[p, me_row] = value
        for d in range(1, ranks):
            gather(p, d, lanes).start()

    def reduce_end(p, lanes=None):
        for d in range(1, ranks):
            gather(p, d, lanes).wait()
        for r in range(ranks):
            zone[r * lines : (r + 1) * lines, :] = full[p, r]

    def set_operand(p, value):
        h, l = split(value)
        operand[p, 0:kp, :] = h
        operand[p, kp:k, :] = l

    for i in range(2):
        set_operand(i, sketch[i * kp : (i + 1) * kp, :])
    acc[...] = jnp.zeros_like(acc)
    gacc[...] = jnp.zeros_like(gacc)
    wait1, wait2 = EARLY * chunks // 16, LATE * chunks // 16

    def step(s, carry):
        @pl.when(s < units)
        def _():
            produce(s // chunks, s % chunks)

        @pl.when(jnp.logical_and(s >= PAIR, s < units + PAIR))
        def _():
            u = s - PAIR
            add_cores(u // chunks, u % chunks)

        @pl.when(jnp.logical_and(s >= PAIR + LEAD, s < units + PAIR + LEAD))
        def _():
            u = s - PAIR - LEAD
            add_chips(u // chunks, u % chunks)

        @pl.when(s >= PAIR + LEAD + BACK)
        def _():
            u = s - PAIR - LEAD - BACK
            accumulate(u // chunks, u % chunks)

        since = s - (chunks - 1 + PAIR + LEAD + BACK)
        done = since // chunks
        at = since % chunks
        live = jnp.logical_and(since >= 0, done < PHASES - 1)

        @pl.when(jnp.logical_and(live, at == 0))
        def _():
            fold_gram()
            reduce_start(done)

        @pl.when(jnp.logical_and(live, at == wait1))
        def _():
            reduce_share(done)

        @pl.when(jnp.logical_and(live, at == wait2))
        def _():
            reduce_end(done)

            @pl.when(done % 2 == 0)
            def _():
                f11 = inverse_factor(zone[:, width : width + kp])
                value = dot_full(f11, zone[:, 0:width], 1, 0)
                lead_factor[...] = f11
                lead[...] = value
                set_operand(2, value)

            @pl.when(done == 1)
            def _():
                l21, rest = below(zone[:, width : width + k], lead_factor[...])
                f22 = inverse_factor(rest)
                value = zone[:, 0:width] - dot_full(l21, lead[...], 1, 0)
                set_operand(3, dot_full(f22, value, 1, 0))

            @pl.when(done == 2)
            def _():
                scaled = lead_factor[...] * scale
                for i, h, at in blocks:
                    value = panel[2, me * per + i, h]
                    basis[0:kp, at : at + HALF] = dot_full(scaled, value, 1, 0)
                basis_copy(0).start()

        return carry

    lax.fori_loop(0, units + PAIR + LEAD + BACK, step, 0)

    fold_gram()
    own_gram = acc[:, width : width + k]
    gram[...] = own_gram
    grams[me_row] = own_gram
    reduce_start(3, width)
    for d in range(1, ranks):
        give_gram(d).start()
    reduce_share(3, width)
    for d in range(1, ranks):
        give_gram(d).wait_recv()
    gram_total = grams[0]
    for r in range(1, ranks):
        gram_total = gram_total + grams[r]
    l21, rest = below(gram_total, lead_factor[...])
    top = lead[...]
    f22 = inverse_factor(rest)
    low_top = dot_full(l21, top, 1, 0)
    for i, h, at in blocks:
        value = panel[3, me * per + i, h]
        basis[kp:k, at : at + HALF] = scale * value - dot_full(l21, basis[0:kp, at : at + HALF], 1, 0)
    reduce_end(3, width)
    sums = jnp.concatenate([top, dot_full(f22, zone[:, 0:width] - low_top, 1, 0)], axis=0)
    coeffs_out[...] = sums
    spect[0] = dot_full(sums, sums, 1, 1)
    for d in range(1, groups):
        share_spectrum(d).start()
    for i, h, at in blocks:
        basis[kp:k, at : at + HALF] = dot_full(f22, basis[kp:k, at : at + HALF], 1, 0)
    basis_copy(1).start()
    for d in range(1, ranks):
        give_gram(d).wait_send()
    for d in range(1, groups):
        share_spectrum(d).wait()
    a = spect[0] + spect[2]
    b = spect[1] + spect[3]
    spectrum_out[...] = (a + b) / batch_total
    for i in range(2):
        basis_copy(i).wait()


def finish(basis, coeffs, spectrum, basis_out, coeffs_out, spectrum_out, hold, rows, tiny, came, went):
    lines = basis.shape[0] // PIECES
    routes = [(coeffs, rows, coeffs_out), (spectrum, tiny, spectrum_out)]
    for i in range(PIECES):
        at = pl.ds(i * lines, lines)
        routes.append((basis.at[at, :], hold.at[at, :], basis_out.at[at, :]))
    loads = [pltpu.make_async_copy(r[0], r[1], came.at[i]) for i, r in enumerate(routes)]
    stores = [pltpu.make_async_copy(r[1], r[2], went.at[i]) for i, r in enumerate(routes)]
    for load in loads:
        load.start()
    for load, store in zip(loads, stores):
        load.wait()
        store.start()
    for store in stores:
        store.wait()


def on_device(stress, sketch):
    rows_dev, width = stress.shape
    k = sketch.shape[0]
    kp = k // 2
    groups = lax.axis_size("snaps")
    ranks = lax.axis_size("rows")
    share = rows_dev // groups
    chunks = rows_dev // CHUNK
    lines = kp // ranks
    wide = width + 128
    scale = math.sqrt(float(rows_dev * ranks))
    vmem = pl.BlockSpec(memory_space=pltpu.VMEM)
    dma = pltpu.SemaphoreType.DMA
    found = pl.pallas_call(
        functools.partial(kernel, ranks, float(width * groups), scale),
        out_shape=(
            jax.ShapeDtypeStruct((k, share), F32),
            jax.ShapeDtypeStruct((k, width), F32),
            jax.ShapeDtypeStruct((k, k), F32),
        ),
        in_specs=[pl.BlockSpec(memory_space=pl.ANY), vmem],
        out_specs=(pl.BlockSpec(memory_space=pl.ANY), vmem, vmem),
        scratch_shapes=[
            pltpu.VMEM((SLOTS, CHUNK, width), F32),
            pltpu.VMEM((rows_dev, width), BF16),
            pltpu.VMEM((rows_dev, width), BF16),
            pltpu.VMEM((PHASES, k, width), BF16),
            pltpu.VMEM((chunks, 2, kp, HALF), F32),
            pltpu.VMEM((PHASES, chunks, kp, HALF), F32),
            pltpu.VMEM((chunks, kp, HALF), F32),
            pltpu.VMEM((PHASES, chunks, kp, HALF), F32),
            pltpu.VMEM((PHASES, chunks, 2, kp, HALF), F32),
            pltpu.VMEM((kp, wide), F32),
            pltpu.VMEM((k, 2 * k), F32),
            pltpu.VMEM((PHASES, ranks, lines, wide), F32),
            pltpu.VMEM((PHASES, ranks, lines, wide), F32),
            pltpu.VMEM((PHASES, lines, wide), F32),
            pltpu.VMEM((PHASES, ranks, lines, wide), F32),
            pltpu.VMEM((kp, wide), F32),
            pltpu.VMEM((kp, width), F32),
            pltpu.VMEM((k, share), F32),
            pltpu.VMEM((groups, k, k), F32),
            pltpu.VMEM((kp, k), F32),
            pltpu.VMEM((ranks, kp, k), F32),
            pltpu.VMEM((kp, kp), F32),
            dma((SLOTS, CUTS)),
            dma((2,)),
            dma((PHASES, chunks)),
            dma((PHASES, chunks)),
            dma((PHASES, chunks)),
            dma((PHASES, chunks)),
            dma((PHASES, chunks)),
            dma((PHASES, chunks)),
            dma((PHASES, ranks)),
            dma((PHASES, ranks)),
            dma((PHASES, ranks)),
            dma((PHASES, ranks)),
            dma((groups,)),
            dma((groups,)),
            dma((ranks,)),
            dma((ranks,)),
        ],
        compiler_params=pltpu.CompilerParams(
            collective_id=0, has_side_effects=True, vmem_limit_bytes=58 * 1024 * 1024
        ),
        cost_estimate=pl.CostEstimate(
            flops=24 * rows_dev * width * k, bytes_accessed=rows_dev * width * 4, transcendentals=0
        ),
    )(stress, sketch)
    anywhere = pl.BlockSpec(memory_space=pl.ANY)
    return pl.pallas_call(
        finish,
        out_shape=tuple(jax.ShapeDtypeStruct(a.shape, a.dtype) for a in found),
        in_specs=[anywhere] * 3,
        out_specs=(anywhere,) * 3,
        scratch_shapes=[
            pltpu.VMEM((k, share), F32),
            pltpu.VMEM((k, width), F32),
            pltpu.VMEM((k, k), F32),
            dma((PIECES + 2,)),
            dma((PIECES + 2,)),
        ],
    )(*found)


def solution(mesh):
    placed = (P("rows", "snaps"), P(None, "snaps"))
    return jax.shard_map(
        on_device,
        mesh=mesh,
        in_specs=placed,
        out_specs=(P(None, ("rows", "snaps")), P(None, "snaps"), P()),
        check_vma=False,
    )
```

```python
import functools
import math

import jax
import jax.numpy as jnp
from jax import lax
from jax.experimental import pallas as pl
from jax.experimental.pallas import tpu as pltpu
from jax.sharding import PartitionSpec as P

MESH = pl.DeviceIdType.MESH
F32 = jnp.float32
BF16 = jnp.bfloat16
CHUNK = 2048
HALF = CHUNK // 2
SLOTS = 3
PIECE = 128
CUTS = 4
PIECES = 4
PHASES = 4
LEAD = 4
EARLY = 1
LATE = 2
PAIR = 1
BACK = 1


def dot(left_m, right_m, left_dim, right_dim, precision=None):
    return lax.dot_general(
        left_m,
        right_m,
        (((left_dim,), (right_dim,)), ((), ())),
        precision=precision,
        preferred_element_type=F32,
    )


def dot_full(left_m, right_m, left_dim, right_dim):
    return dot(left_m, right_m, left_dim, right_dim, lax.Precision.HIGHEST)


def split(value):
    high = value.astype(BF16)
    low = (value - high.astype(F32)).astype(BF16)
    return high, low


def inverse_factor(gram):
    k = gram.shape[0]
    line = lax.broadcasted_iota(jnp.int32, (k, k), 0)
    lane = lax.broadcasted_iota(jnp.int32, (k, k), 1)
    wide_line = lax.broadcasted_iota(jnp.int32, (k, 2 * k), 0)
    ident = jnp.where(line == lane, 1.0, 0.0).astype(F32)
    table = jnp.concatenate([gram, ident], axis=1)
    for j in range(0, k, 2):
        column0 = jnp.broadcast_to(table[:, j : j + 1], (k, 2 * k))
        column1 = jnp.broadcast_to(table[:, j + 1 : j + 2], (k, 2 * k))
        pivot0 = column0[j : j + 1]
        under = column0[j + 1 : j + 2]
        beside = column1[j : j + 1] / pivot0
        pivot1 = column1[j + 1 : j + 2] - under * beside
        row0 = table[j : j + 1] / pivot0
        row1 = (table[j + 1 : j + 2] - under * row0) / pivot1
        column1 = jnp.where(wide_line > j + 1, column1 - column0 * beside, 0.0)
        column0 = jnp.where(wide_line > j, column0, 0.0)
        table = table - column0 * row0 - column1 * row1
    diag = jnp.sum(jnp.where(line == lane, table[:, :k], 0.0), axis=1, keepdims=True)
    return table[:, k:] / jnp.sqrt(diag)


def below(gram, f11):
    h = f11.shape[0]
    l21 = dot_full(gram[:, 0:h], f11, 1, 1)
    return l21, gram[:, h : 2 * h] - dot_full(l21, l21, 1, 1)


def kernel(
    ranks, batch_total, scale,
    stress, sketch, basis_out, coeffs_out, spectrum_out,
    stage, high, low, operand, part, got1, summed, got2, panel,
    acc, gacc, spread, landed, total, full, zone, lead, basis, held, sums, spectrum, spect, gram, grams, lead_factor,
    stage_sem, small_sem, basis_sem, send1, recv1, send2, recv2, send3, recv3,
    rs_send, rs_recv, ag_send, ag_recv, sp_send, sp_recv, gr_send, gr_recv,
):
    groups = 4
    k = sketch.shape[0]
    kp = k // 2
    width = stress.shape[1]
    chunks = summed.shape[0]
    lines = kp // ranks
    me_row = lax.axis_index("rows")
    me = lax.axis_index("snaps")
    mine = me % 2
    core = me + 1 - 2 * mine
    chip = (me + 2) % groups
    units = PHASES * chunks
    per = chunks // groups
    blocks = [(i, h, (2 * i + h) * HALF) for i in range(per) for h in range(2)]

    def load(c, q):
        slot = c % SLOTS
        rows = CHUNK // CUTS
        return pltpu.make_async_copy(
            stress.at[pl.ds(c * CHUNK + q * rows, rows), :],
            stage.at[slot, pl.ds(q * rows, rows), :],
            stage_sem.at[slot, q],
        )

    sketch_copy = pltpu.make_async_copy(sketch, held, small_sem.at[0])
    coeffs_copy = pltpu.make_async_copy(sums, coeffs_out, small_sem.at[1])
    spectrum_copy = pltpu.make_async_copy(spectrum, spectrum_out, small_sem.at[2])
    load(0, 0).start()
    sketch_copy.start()
    for q in range(1, CUTS):
        load(0, q).start()

    barrier = pltpu.get_barrier_semaphore()
    for d in range(1, ranks):
        pl.semaphore_signal(
            barrier, inc=1, device_id={"rows": (me_row + d) % ranks}, device_id_type=MESH
        )
    for d in range(1, groups):
        pl.semaphore_signal(
            barrier, inc=1, device_id={"snaps": (me + d) % groups}, device_id_type=MESH
        )

    def remote(src, dst, s_sem, r_sem, device):
        return pltpu.make_async_remote_copy(
            src_ref=src, dst_ref=dst, send_sem=s_sem, recv_sem=r_sem,
            device_id=device, device_id_type=MESH,
        )

    def hop1(p, c):
        return remote(
            part.at[c, 1 - mine], got1.at[p, c], send1.at[p, c], recv1.at[p, c],
            {"snaps": core},
        )

    def hop2(p, c):
        return remote(summed.at[c], got2.at[p, c], send2.at[p, c], recv2.at[p, c], {"snaps": chip})

    def hop3(p, c):
        return remote(
            panel.at[p, c, mine], panel.at[p, c, mine], send3.at[p, c], recv3.at[p, c],
            {"snaps": core},
        )

    def scatter(p, d, lanes=None):
        to = (me_row + d) % ranks
        src, dst = spread.at[p, to], landed.at[p, d]
        if lanes is not None:
            src, dst = src.at[:, 0:lanes], dst.at[:, 0:lanes]
        return remote(src, dst, rs_send.at[p, d], rs_recv.at[p, d], {"rows": to})

    def gather(p, d, lanes=None):
        to = (me_row + d) % ranks
        src, dst = total.at[p], full.at[p, me_row]
        if lanes is not None:
            src, dst = src.at[:, 0:lanes], dst.at[:, 0:lanes]
        return remote(src, dst, ag_send.at[p, d], ag_recv.at[p, d], {"rows": to})

    def give_gram(d):
        return remote(
            gram, grams.at[me_row], gr_send.at[d], gr_recv.at[d], {"rows": (me_row + d) % ranks}
        )

    def share_spectrum(d):
        return remote(
            spect.at[0], spect.at[d], sp_send.at[d], sp_recv.at[d], {"snaps": (me + d) % groups}
        )

    def basis_copy(i):
        at = pl.ds(i * kp, kp)
        return pltpu.make_async_copy(basis.at[at, :], basis_out.at[at, :], basis_sem.at[i])

    def convert(c):
        slot = c % SLOTS

        @pl.when(c + 1 < chunks)
        def _():
            for q in range(CUTS):
                load(c + 1, q).start()

        per_cut = CHUNK // CUTS // PIECE
        for q in range(CUTS):
            load(c, q).wait()

            def body(i, carry):
                h, l = split(stage[slot, pl.ds(i * PIECE, PIECE), :])
                at = pl.ds(c * CHUNK + i * PIECE, PIECE)
                high[at, :] = h
                low[at, :] = l
                return carry

            lax.fori_loop(q * per_cut, (q + 1) * per_cut, body, 0, unroll=True)

    def project(p, c, h):
        at = pl.ds(c * CHUNK + h * HALF, HALF)
        both = dot(operand[p], high[at, :], 1, 1)
        rest = dot(operand[p, 0:kp, :], low[at, :], 1, 1)
        part[c, h] = both[0:kp] + (both[kp:k] + rest)

    def produce(p, c):
        @pl.when(p == 0)
        def _():
            convert(c)

        project(p, c, 1 - mine)

        @pl.when(jnp.logical_and(p == 0, c == 0))
        def _():
            pl.semaphore_wait(barrier, ranks - 1 + groups - 1)

        hop1(p, c).start()
        project(p, c, mine)

    def add_cores(p, c):
        hop1(p, c).wait()
        summed[c] = part[c, mine] + got1[p, c]
        hop2(p, c).start()

    def add_chips(p, c):
        hop2(p, c).wait()
        panel[p, c, mine] = summed[c] + got2[p, c]
        hop3(p, c).start()

    def stacked(p, c):
        value = jnp.concatenate([panel[p, c, 0], panel[p, c, 1]], axis=1)
        hi, lo = split(value)
        return jnp.concatenate([hi, lo], axis=0)

    def accumulate(p, c):
        hop3(p, c).wait()
        stack = stacked(p, c)
        at = pl.ds(c * CHUNK, CHUNK)
        both = dot(stack, high[at, :], 1, 0)
        rest = dot(stack[0:kp], low[at, :], 1, 0)
        acc[:, 0:width] += both[0:kp] + (both[kp:k] + rest)

        @pl.when(p % 2 == 0)
        def _():
            gacc[:, 0:k] += dot(stack, stack, 1, 1)

        @pl.when(p % 2 == 1)
        def _():
            gacc[...] += dot(stack, jnp.concatenate([stacked(p - 1, c), stack], axis=0), 1, 1)

    def fold_gram():
        rows = gacc[0:kp, :] + gacc[kp:k, :]
        for i in range(2):
            at = i * k
            acc[:, width + i * kp : width + (i + 1) * kp] = (
                rows[:, at : at + kp] + rows[:, at + kp : at + k]
            )
        gacc[...] = jnp.zeros_like(gacc)

    def reduce_start(p, lanes=None):
        for r in range(ranks):
            spread[p, r] = acc[r * lines : (r + 1) * lines, :]
        acc[...] = jnp.zeros_like(acc)
        for d in range(1, ranks):
            scatter(p, d, lanes).start()

    def reduce_share(p, lanes=None):
        value = spread[p, me_row]
        for d in range(1, ranks):
            scatter(p, d, lanes).wait()
            value = value + landed[p, d]
        total[p] = value
        full[p, me_row] = value
        for d in range(1, ranks):
            gather(p, d, lanes).start()

    def reduce_end(p, lanes=None):
        for d in range(1, ranks):
            gather(p, d, lanes).wait()
        for r in range(ranks):
            zone[r * lines : (r + 1) * lines, :] = full[p, r]

    def set_operand(p, value):
        h, l = split(value)
        operand[p, 0:kp, :] = h
        operand[p, kp:k, :] = l

    acc[...] = jnp.zeros_like(acc)
    gacc[...] = jnp.zeros_like(gacc)
    sketch_copy.wait()
    for i in range(2):
        set_operand(i, held[i * kp : (i + 1) * kp, :])

    def step(s, carry):
        @pl.when(s < units)
        def _():
            produce(s // chunks, s % chunks)

        @pl.when(jnp.logical_and(s >= PAIR, s < units + PAIR))
        def _():
            u = s - PAIR
            add_cores(u // chunks, u % chunks)

        @pl.when(jnp.logical_and(s >= PAIR + LEAD, s < units + PAIR + LEAD))
        def _():
            u = s - PAIR - LEAD
            add_chips(u // chunks, u % chunks)

        @pl.when(s >= PAIR + LEAD + BACK)
        def _():
            u = s - PAIR - LEAD - BACK
            accumulate(u // chunks, u % chunks)

        since = s - (chunks - 1 + PAIR + LEAD + BACK)
        done = since // chunks
        at = since % chunks
        live = jnp.logical_and(since >= 0, done < PHASES - 1)

        @pl.when(jnp.logical_and(live, at == 0))
        def _():
            fold_gram()
            reduce_start(done)

        @pl.when(jnp.logical_and(live, at == EARLY))
        def _():
            reduce_share(done)

        @pl.when(jnp.logical_and(live, at == LATE))
        def _():
            reduce_end(done)

            @pl.when(done % 2 == 0)
            def _():
                f11 = inverse_factor(zone[:, width : width + kp])
                value = dot_full(f11, zone[:, 0:width], 1, 0)
                lead_factor[...] = f11
                lead[...] = value
                set_operand(2, value)

            @pl.when(done == 1)
            def _():
                l21, rest = below(zone[:, width : width + k], lead_factor[...])
                f22 = inverse_factor(rest)
                value = zone[:, 0:width] - dot_full(l21, lead[...], 1, 0)
                set_operand(3, dot_full(f22, value, 1, 0))

            @pl.when(done == 2)
            def _():
                scaled = lead_factor[...] * scale
                for i, h, at in blocks:
                    value = panel[2, me * per + i, h]
                    basis[0:kp, at : at + HALF] = dot_full(scaled, value, 1, 0)
                basis_copy(0).start()

        return carry

    lax.fori_loop(0, units + PAIR + LEAD + BACK, step, 0)

    reduce_start(3, width)
    fold_gram()
    own_gram = acc[:, width : width + k]
    gram[...] = own_gram
    grams[me_row] = own_gram
    for d in range(1, ranks):
        give_gram(d).start()
    reduce_share(3, width)
    for d in range(1, ranks):
        give_gram(d).wait_recv()
    gram_total = grams[0]
    for r in range(1, ranks):
        gram_total = gram_total + grams[r]
    l21, rest = below(gram_total, lead_factor[...])
    top = lead[...]
    f22 = inverse_factor(rest)
    low_top = dot_full(l21, top, 1, 0)
    reduce_end(3, width)
    found = jnp.concatenate([top, dot_full(f22, zone[:, 0:width] - low_top, 1, 0)], axis=0)
    sums[...] = found
    spect[0] = dot_full(found, found, 1, 1)
    for d in range(1, groups):
        share_spectrum(d).start()
    coeffs_copy.start()
    for i, h, at in blocks:
        value = panel[3, me * per + i, h]
        basis[kp:k, at : at + HALF] = scale * value - dot_full(l21, basis[0:kp, at : at + HALF], 1, 0)
    for i, h, at in blocks:
        basis[kp:k, at : at + HALF] = dot_full(f22, basis[kp:k, at : at + HALF], 1, 0)
    basis_copy(1).start()
    for d in range(1, ranks):
        give_gram(d).wait_send()
    for d in range(1, groups):
        share_spectrum(d).wait()
    a = spect[0] + spect[2]
    b = spect[1] + spect[3]
    spectrum[...] = (a + b) / batch_total
    spectrum_copy.start()
    coeffs_copy.wait()
    for i in range(2):
        basis_copy(i).wait()
    spectrum_copy.wait()


def finish(basis, coeffs, spectrum, basis_out, coeffs_out, spectrum_out, hold, rows, tiny, came, went):
    lines = basis.shape[0] // PIECES
    routes = [(coeffs, rows, coeffs_out), (spectrum, tiny, spectrum_out)]
    for i in range(PIECES):
        at = pl.ds(i * lines, lines)
        routes.append((basis.at[at, :], hold.at[at, :], basis_out.at[at, :]))
    loads = [pltpu.make_async_copy(r[0], r[1], came.at[i]) for i, r in enumerate(routes)]
    stores = [pltpu.make_async_copy(r[1], r[2], went.at[i]) for i, r in enumerate(routes)]
    for load in loads:
        load.start()
    for load, store in zip(loads, stores):
        load.wait()
        store.start()
    for store in stores:
        store.wait()


def on_device(stress, sketch):
    rows_dev, width = stress.shape
    k = sketch.shape[0]
    kp = k // 2
    groups = lax.axis_size("snaps")
    ranks = lax.axis_size("rows")
    share = rows_dev // groups
    chunks = rows_dev // CHUNK
    lines = kp // ranks
    wide = width + 128
    scale = math.sqrt(float(rows_dev * ranks))
    anywhere = pl.BlockSpec(memory_space=pl.ANY)
    dma = pltpu.SemaphoreType.DMA
    found = pl.pallas_call(
        functools.partial(kernel, ranks, float(width * groups), scale),
        out_shape=(
            jax.ShapeDtypeStruct((k, share), F32),
            jax.ShapeDtypeStruct((k, width), F32),
            jax.ShapeDtypeStruct((k, k), F32),
        ),
        in_specs=[anywhere] * 2,
        out_specs=(anywhere,) * 3,
        scratch_shapes=[
            pltpu.VMEM((SLOTS, CHUNK, width), F32),
            pltpu.VMEM((rows_dev, width), BF16),
            pltpu.VMEM((rows_dev, width), BF16),
            pltpu.VMEM((PHASES, k, width), BF16),
            pltpu.VMEM((chunks, 2, kp, HALF), F32),
            pltpu.VMEM((PHASES, chunks, kp, HALF), F32),
            pltpu.VMEM((chunks, kp, HALF), F32),
            pltpu.VMEM((PHASES, chunks, kp, HALF), F32),
            pltpu.VMEM((PHASES, chunks, 2, kp, HALF), F32),
            pltpu.VMEM((kp, wide), F32),
            pltpu.VMEM((k, 2 * k), F32),
            pltpu.VMEM((PHASES, ranks, lines, wide), F32),
            pltpu.VMEM((PHASES, ranks, lines, wide), F32),
            pltpu.VMEM((PHASES, lines, wide), F32),
            pltpu.VMEM((PHASES, ranks, lines, wide), F32),
            pltpu.VMEM((kp, wide), F32),
            pltpu.VMEM((kp, width), F32),
            pltpu.VMEM((k, share), F32),
            pltpu.VMEM((k, width), F32),
            pltpu.VMEM((k, width), F32),
            pltpu.VMEM((k, k), F32),
            pltpu.VMEM((groups, k, k), F32),
            pltpu.VMEM((kp, k), F32),
            pltpu.VMEM((ranks, kp, k), F32),
            pltpu.VMEM((kp, kp), F32),
            dma((SLOTS, CUTS)),
            dma((3,)),
            dma((2,)),
            dma((PHASES, chunks)),
            dma((PHASES, chunks)),
            dma((PHASES, chunks)),
            dma((PHASES, chunks)),
            dma((PHASES, chunks)),
            dma((PHASES, chunks)),
            dma((PHASES, ranks)),
            dma((PHASES, ranks)),
            dma((PHASES, ranks)),
            dma((PHASES, ranks)),
            dma((groups,)),
            dma((groups,)),
            dma((ranks,)),
            dma((ranks,)),
        ],
        compiler_params=pltpu.CompilerParams(
            collective_id=0, has_side_effects=True, vmem_limit_bytes=58 * 1024 * 1024
        ),
        cost_estimate=pl.CostEstimate(
            flops=24 * rows_dev * width * k, bytes_accessed=rows_dev * width * 4, transcendentals=0
        ),
    )(stress, sketch)
    return pl.pallas_call(
        finish,
        out_shape=tuple(jax.ShapeDtypeStruct(a.shape, a.dtype) for a in found),
        in_specs=[anywhere] * 3,
        out_specs=(anywhere,) * 3,
        scratch_shapes=[
            pltpu.VMEM((k, share), F32),
            pltpu.VMEM((k, width), F32),
            pltpu.VMEM((k, k), F32),
            dma((PIECES + 2,)),
            dma((PIECES + 2,)),
        ],
    )(*found)


def solution(mesh):
    placed = (P("rows", "snaps"), P(None, "snaps"))
    return jax.shard_map(
        on_device,
        mesh=mesh,
        in_specs=placed,
        out_specs=(P(None, ("rows", "snaps")), P(None, "snaps"), P()),
        check_vma=False,
    )
```

```python
import functools
import math

import jax
import jax.numpy as jnp
from jax import lax
from jax.experimental import pallas as pl
from jax.experimental.pallas import tpu as pltpu
from jax.sharding import PartitionSpec as P

MESH = pl.DeviceIdType.MESH
F32 = jnp.float32
BF16 = jnp.bfloat16
CHUNK = 2048
HALF = CHUNK // 2
SLOTS = 3
PIECE = 128
CUTS = 4
PIECES = 2
PHASES = 4
LEAD = 4
EARLY = 1
LATE = 2
PAIR = 1
BACK = 1


def dot(left_m, right_m, left_dim, right_dim, precision=None):
    return lax.dot_general(
        left_m,
        right_m,
        (((left_dim,), (right_dim,)), ((), ())),
        precision=precision,
        preferred_element_type=F32,
    )


def dot_full(left_m, right_m, left_dim, right_dim):
    return dot(left_m, right_m, left_dim, right_dim, lax.Precision.HIGHEST)


def split(value):
    high = value.astype(BF16)
    low = (value - high.astype(F32)).astype(BF16)
    return high, low


def inverse_factor(gram):
    k = gram.shape[0]
    line = lax.broadcasted_iota(jnp.int32, (k, k), 0)
    lane = lax.broadcasted_iota(jnp.int32, (k, k), 1)
    wide_line = lax.broadcasted_iota(jnp.int32, (k, 2 * k), 0)
    ident = jnp.where(line == lane, 1.0, 0.0).astype(F32)
    table = jnp.concatenate([gram, ident], axis=1)
    for j in range(0, k, 2):
        column0 = jnp.broadcast_to(table[:, j : j + 1], (k, 2 * k))
        column1 = jnp.broadcast_to(table[:, j + 1 : j + 2], (k, 2 * k))
        pivot0 = column0[j : j + 1]
        under = column0[j + 1 : j + 2]
        beside = column1[j : j + 1] / pivot0
        pivot1 = column1[j + 1 : j + 2] - under * beside
        row0 = table[j : j + 1] / pivot0
        row1 = (table[j + 1 : j + 2] - under * row0) / pivot1
        column1 = jnp.where(wide_line > j + 1, column1 - column0 * beside, 0.0)
        column0 = jnp.where(wide_line > j, column0, 0.0)
        table = table - column0 * row0 - column1 * row1
    diag = jnp.sum(jnp.where(line == lane, table[:, :k], 0.0), axis=1, keepdims=True)
    return table[:, k:] / jnp.sqrt(diag)


def below(gram, f11):
    h = f11.shape[0]
    l21 = dot_full(gram[:, 0:h], f11, 1, 1)
    return l21, gram[:, h : 2 * h] - dot_full(l21, l21, 1, 1)


def kernel(
    ranks, batch_total, scale,
    stress, sketch, basis_out, coeffs_out, spectrum_out,
    stage, high, low, operand, part, got1, summed, got2, panel,
    acc, gacc, spread, landed, total, full, zone, lead, basis, held, sums, spectrum, spect, gram, grams, lead_factor,
    stage_sem, small_sem, basis_sem, send1, recv1, send2, recv2, send3, recv3,
    rs_send, rs_recv, ag_send, ag_recv, sp_send, sp_recv, gr_send, gr_recv,
):
    groups = 4
    k = sketch.shape[0]
    kp = k // 2
    width = stress.shape[1]
    chunks = summed.shape[0]
    lines = kp // ranks
    me_row = lax.axis_index("rows")
    me = lax.axis_index("snaps")
    mine = me % 2
    core = me + 1 - 2 * mine
    chip = (me + 2) % groups
    units = PHASES * chunks
    per = chunks // groups
    blocks = [(i, h, (2 * i + h) * HALF) for i in range(per) for h in range(2)]

    def load(c, q):
        slot = c % SLOTS
        rows = CHUNK // CUTS
        return pltpu.make_async_copy(
            stress.at[pl.ds(c * CHUNK + q * rows, rows), :],
            stage.at[slot, pl.ds(q * rows, rows), :],
            stage_sem.at[slot, q],
        )

    sketch_copy = pltpu.make_async_copy(sketch, held, small_sem.at[0])
    coeffs_copy = pltpu.make_async_copy(sums, coeffs_out, small_sem.at[1])
    spectrum_copy = pltpu.make_async_copy(spectrum, spectrum_out, small_sem.at[2])
    load(0, 0).start()
    sketch_copy.start()
    for q in range(1, CUTS):
        load(0, q).start()

    barrier = pltpu.get_barrier_semaphore()
    for d in range(1, ranks):
        pl.semaphore_signal(
            barrier, inc=1, device_id={"rows": (me_row + d) % ranks}, device_id_type=MESH
        )
    for d in range(1, groups):
        pl.semaphore_signal(
            barrier, inc=1, device_id={"snaps": (me + d) % groups}, device_id_type=MESH
        )

    def remote(src, dst, s_sem, r_sem, device):
        return pltpu.make_async_remote_copy(
            src_ref=src, dst_ref=dst, send_sem=s_sem, recv_sem=r_sem,
            device_id=device, device_id_type=MESH,
        )

    def hop1(p, c):
        return remote(
            part.at[c, 1 - mine], got1.at[p, c], send1.at[p, c], recv1.at[p, c],
            {"snaps": core},
        )

    def hop2(p, c):
        return remote(summed.at[c], got2.at[p, c], send2.at[p, c], recv2.at[p, c], {"snaps": chip})

    def hop3(p, c):
        return remote(
            panel.at[p, c, mine], panel.at[p, c, mine], send3.at[p, c], recv3.at[p, c],
            {"snaps": core},
        )

    def scatter(p, d, lanes=None):
        to = (me_row + d) % ranks
        src, dst = spread.at[p, to], landed.at[p, d]
        if lanes is not None:
            src, dst = src.at[:, 0:lanes], dst.at[:, 0:lanes]
        return remote(src, dst, rs_send.at[p, d], rs_recv.at[p, d], {"rows": to})

    def gather(p, d, lanes=None):
        to = (me_row + d) % ranks
        src, dst = total.at[p], full.at[p, me_row]
        if lanes is not None:
            src, dst = src.at[:, 0:lanes], dst.at[:, 0:lanes]
        return remote(src, dst, ag_send.at[p, d], ag_recv.at[p, d], {"rows": to})

    def give_gram(d):
        return remote(
            gram, grams.at[me_row], gr_send.at[d], gr_recv.at[d], {"rows": (me_row + d) % ranks}
        )

    def share_spectrum(d):
        return remote(
            spect.at[0], spect.at[d], sp_send.at[d], sp_recv.at[d], {"snaps": (me + d) % groups}
        )

    def basis_copy(i):
        at = pl.ds(i * kp, kp)
        return pltpu.make_async_copy(basis.at[at, :], basis_out.at[at, :], basis_sem.at[i])

    def convert(c):
        slot = c % SLOTS

        @pl.when(c + 1 < chunks)
        def _():
            for q in range(CUTS):
                load(c + 1, q).start()

        per_cut = CHUNK // CUTS // PIECE
        for q in range(CUTS):
            load(c, q).wait()

            def body(i, carry):
                h, l = split(stage[slot, pl.ds(i * PIECE, PIECE), :])
                at = pl.ds(c * CHUNK + i * PIECE, PIECE)
                high[at, :] = h
                low[at, :] = l
                return carry

            lax.fori_loop(q * per_cut, (q + 1) * per_cut, body, 0, unroll=True)

    def project(p, c, h):
        at = pl.ds(c * CHUNK + h * HALF, HALF)
        both = dot(operand[p], high[at, :], 1, 1)
        rest = dot(operand[p, 0:kp, :], low[at, :], 1, 1)
        part[c, h] = both[0:kp] + (both[kp:k] + rest)

    def produce(p, c):
        @pl.when(p == 0)
        def _():
            convert(c)

        project(p, c, 1 - mine)

        @pl.when(jnp.logical_and(p == 0, c == 0))
        def _():
            pl.semaphore_wait(barrier, ranks - 1 + groups - 1)

        hop1(p, c).start()
        project(p, c, mine)

    def add_cores(p, c):
        hop1(p, c).wait()
        summed[c] = part[c, mine] + got1[p, c]
        hop2(p, c).start()

    def add_chips(p, c):
        hop2(p, c).wait()
        panel[p, c, mine] = summed[c] + got2[p, c]
        hop3(p, c).start()

    def stacked(p, c, h):
        hi, lo = split(panel[p, c, h])
        return jnp.concatenate([hi, lo], axis=0)

    def accumulate(p, c, h):
        stack = stacked(p, c, h)
        at = pl.ds(c * CHUNK + h * HALF, HALF)
        both = dot(stack, high[at, :], 1, 0)
        rest = dot(stack[0:kp], low[at, :], 1, 0)
        acc[:, 0:width] += both[0:kp] + (both[kp:k] + rest)

        @pl.when(p % 2 == 0)
        def _():
            gacc[:, 0:k] += dot(stack, stack, 1, 1)

        @pl.when(p % 2 == 1)
        def _():
            gacc[...] += dot(stack, jnp.concatenate([stacked(p - 1, c, h), stack], axis=0), 1, 1)

    def fold_gram():
        rows = gacc[0:kp, :] + gacc[kp:k, :]
        for i in range(2):
            at = i * k
            acc[:, width + i * kp : width + (i + 1) * kp] = (
                rows[:, at : at + kp] + rows[:, at + kp : at + k]
            )
        gacc[...] = jnp.zeros_like(gacc)

    def reduce_start(p, lanes=None):
        for r in range(ranks):
            spread[p, r] = acc[r * lines : (r + 1) * lines, :]
        acc[...] = jnp.zeros_like(acc)
        for d in range(1, ranks):
            scatter(p, d, lanes).start()

    def reduce_share(p, lanes=None):
        value = spread[p, me_row]
        for d in range(1, ranks):
            scatter(p, d, lanes).wait()
            value = value + landed[p, d]
        total[p] = value
        full[p, me_row] = value
        for d in range(1, ranks):
            gather(p, d, lanes).start()

    def reduce_end(p, lanes=None):
        for d in range(1, ranks):
            gather(p, d, lanes).wait()
        for r in range(ranks):
            zone[r * lines : (r + 1) * lines, :] = full[p, r]

    def set_operand(p, value):
        h, l = split(value)
        operand[p, 0:kp, :] = h
        operand[p, kp:k, :] = l

    acc[...] = jnp.zeros_like(acc)
    gacc[...] = jnp.zeros_like(gacc)
    sketch_copy.wait()
    for i in range(2):
        set_operand(i, held[i * kp : (i + 1) * kp, :])

    def step(s, carry):
        @pl.when(s < units)
        def _():
            produce(s // chunks, s % chunks)

        @pl.when(jnp.logical_and(s >= PAIR, s < units + PAIR))
        def _():
            u = s - PAIR
            add_cores(u // chunks, u % chunks)

        @pl.when(jnp.logical_and(s >= PAIR + LEAD, s < units + PAIR + LEAD))
        def _():
            u = s - PAIR - LEAD
            add_chips(u // chunks, u % chunks)

        @pl.when(s >= PAIR + LEAD + BACK)
        def _():
            u = s - PAIR - LEAD - BACK
            p, c = u // chunks, u % chunks
            hop3(p, c).wait()
            accumulate(p, c, 1 - mine)

        since = s - (chunks - 1 + PAIR + LEAD + BACK)
        done = since // chunks
        at = since % chunks
        live = jnp.logical_and(since >= 0, done < PHASES - 1)

        @pl.when(jnp.logical_and(live, at == 0))
        def _():
            fold_gram()
            reduce_start(done)

        @pl.when(jnp.logical_and(live, at == EARLY))
        def _():
            reduce_share(done)

        @pl.when(jnp.logical_and(live, at == LATE))
        def _():
            reduce_end(done)

            @pl.when(done % 2 == 0)
            def _():
                f11 = inverse_factor(zone[:, width : width + kp])
                value = dot_full(f11, zone[:, 0:width], 1, 0)
                lead_factor[...] = f11
                lead[...] = value
                set_operand(2, value)

            @pl.when(done == 1)
            def _():
                l21, rest = below(zone[:, width : width + k], lead_factor[...])
                f22 = inverse_factor(rest)
                value = zone[:, 0:width] - dot_full(l21, lead[...], 1, 0)
                set_operand(3, dot_full(f22, value, 1, 0))

            @pl.when(done == 2)
            def _():
                scaled = lead_factor[...] * scale
                for i, h, at in blocks:
                    value = panel[2, me * per + i, h]
                    basis[0:kp, at : at + HALF] = dot_full(scaled, value, 1, 0)
                basis_copy(0).start()

        @pl.when(jnp.logical_and(s >= PAIR + LEAD, s < units + PAIR + LEAD))
        def _():
            u = s - PAIR - LEAD
            accumulate(u // chunks, u % chunks, mine)

        return carry

    lax.fori_loop(0, units + PAIR + LEAD + BACK, step, 0)

    reduce_start(3, width)
    fold_gram()
    own_gram = acc[:, width : width + k]
    gram[...] = own_gram
    grams[me_row] = own_gram
    for d in range(1, ranks):
        give_gram(d).start()
    reduce_share(3, width)
    for d in range(1, ranks):
        give_gram(d).wait_recv()
    gram_total = grams[0]
    for r in range(1, ranks):
        gram_total = gram_total + grams[r]
    l21, rest = below(gram_total, lead_factor[...])
    top = lead[...]
    f22 = inverse_factor(rest)
    low_top = dot_full(l21, top, 1, 0)
    reduce_end(3, width)
    found = jnp.concatenate([top, dot_full(f22, zone[:, 0:width] - low_top, 1, 0)], axis=0)
    sums[...] = found
    spect[0] = dot_full(found, found, 1, 1)
    for d in range(1, groups):
        share_spectrum(d).start()
    coeffs_copy.start()
    for i, h, at in blocks:
        value = panel[3, me * per + i, h]
        basis[kp:k, at : at + HALF] = scale * value - dot_full(l21, basis[0:kp, at : at + HALF], 1, 0)
    for i, h, at in blocks:
        basis[kp:k, at : at + HALF] = dot_full(f22, basis[kp:k, at : at + HALF], 1, 0)
    basis_copy(1).start()
    for d in range(1, ranks):
        give_gram(d).wait_send()
    for d in range(1, groups):
        share_spectrum(d).wait()
    a = spect[0] + spect[2]
    b = spect[1] + spect[3]
    spectrum[...] = (a + b) / batch_total
    spectrum_copy.start()
    coeffs_copy.wait()
    for i in range(2):
        basis_copy(i).wait()
    spectrum_copy.wait()


def finish(basis, coeffs, spectrum, basis_out, coeffs_out, spectrum_out, hold, rows, tiny, came, went):
    lines = basis.shape[0] // PIECES
    routes = [(coeffs, rows, coeffs_out), (spectrum, tiny, spectrum_out)]
    for i in range(PIECES):
        at = pl.ds(i * lines, lines)
        routes.append((basis.at[at, :], hold.at[at, :], basis_out.at[at, :]))
    loads = [pltpu.make_async_copy(r[0], r[1], came.at[i]) for i, r in enumerate(routes)]
    stores = [pltpu.make_async_copy(r[1], r[2], went.at[i]) for i, r in enumerate(routes)]
    for load in loads:
        load.start()
    for load, store in zip(loads, stores):
        load.wait()
        store.start()
    for store in stores:
        store.wait()


def on_device(stress, sketch):
    rows_dev, width = stress.shape
    k = sketch.shape[0]
    kp = k // 2
    groups = lax.axis_size("snaps")
    ranks = lax.axis_size("rows")
    share = rows_dev // groups
    chunks = rows_dev // CHUNK
    lines = kp // ranks
    wide = width + 128
    scale = math.sqrt(float(rows_dev * ranks))
    anywhere = pl.BlockSpec(memory_space=pl.ANY)
    dma = pltpu.SemaphoreType.DMA
    found = pl.pallas_call(
        functools.partial(kernel, ranks, float(width * groups), scale),
        out_shape=(
            jax.ShapeDtypeStruct((k, share), F32),
            jax.ShapeDtypeStruct((k, width), F32),
            jax.ShapeDtypeStruct((k, k), F32),
        ),
        in_specs=[anywhere] * 2,
        out_specs=(anywhere,) * 3,
        scratch_shapes=[
            pltpu.VMEM((SLOTS, CHUNK, width), F32),
            pltpu.VMEM((rows_dev, width), BF16),
            pltpu.VMEM((rows_dev, width), BF16),
            pltpu.VMEM((PHASES, k, width), BF16),
            pltpu.VMEM((chunks, 2, kp, HALF), F32),
            pltpu.VMEM((PHASES, chunks, kp, HALF), F32),
            pltpu.VMEM((chunks, kp, HALF), F32),
            pltpu.VMEM((PHASES, chunks, kp, HALF), F32),
            pltpu.VMEM((PHASES, chunks, 2, kp, HALF), F32),
            pltpu.VMEM((kp, wide), F32),
            pltpu.VMEM((k, 2 * k), F32),
            pltpu.VMEM((PHASES, ranks, lines, wide), F32),
            pltpu.VMEM((PHASES, ranks, lines, wide), F32),
            pltpu.VMEM((PHASES, lines, wide), F32),
            pltpu.VMEM((PHASES, ranks, lines, wide), F32),
            pltpu.VMEM((kp, wide), F32),
            pltpu.VMEM((kp, width), F32),
            pltpu.VMEM((k, share), F32),
            pltpu.VMEM((k, width), F32),
            pltpu.VMEM((k, width), F32),
            pltpu.VMEM((k, k), F32),
            pltpu.VMEM((groups, k, k), F32),
            pltpu.VMEM((kp, k), F32),
            pltpu.VMEM((ranks, kp, k), F32),
            pltpu.VMEM((kp, kp), F32),
            dma((SLOTS, CUTS)),
            dma((3,)),
            dma((2,)),
            dma((PHASES, chunks)),
            dma((PHASES, chunks)),
            dma((PHASES, chunks)),
            dma((PHASES, chunks)),
            dma((PHASES, chunks)),
            dma((PHASES, chunks)),
            dma((PHASES, ranks)),
            dma((PHASES, ranks)),
            dma((PHASES, ranks)),
            dma((PHASES, ranks)),
            dma((groups,)),
            dma((groups,)),
            dma((ranks,)),
            dma((ranks,)),
        ],
        compiler_params=pltpu.CompilerParams(
            collective_id=0, has_side_effects=True, vmem_limit_bytes=58 * 1024 * 1024
        ),
        cost_estimate=pl.CostEstimate(
            flops=24 * rows_dev * width * k, bytes_accessed=rows_dev * width * 4, transcendentals=0
        ),
    )(stress, sketch)
    return pl.pallas_call(
        finish,
        out_shape=tuple(jax.ShapeDtypeStruct(a.shape, a.dtype) for a in found),
        in_specs=[anywhere] * 3,
        out_specs=(anywhere,) * 3,
        scratch_shapes=[
            pltpu.VMEM((k, share), F32),
            pltpu.VMEM((k, width), F32),
            pltpu.VMEM((k, k), F32),
            dma((PIECES + 2,)),
            dma((PIECES + 2,)),
        ],
    )(*found)


def solution(mesh):
    placed = (P("rows", "snaps"), P(None, "snaps"))
    return jax.shard_map(
        on_device,
        mesh=mesh,
        in_specs=placed,
        out_specs=(P(None, ("rows", "snaps")), P(None, "snaps"), P()),
        check_vma=False,
    )
```

```python
import functools
import math

import jax
import jax.numpy as jnp
from jax import lax
from jax.experimental import pallas as pl
from jax.experimental.pallas import tpu as pltpu
from jax.sharding import PartitionSpec as P

MESH = pl.DeviceIdType.MESH
F32 = jnp.float32
BF16 = jnp.bfloat16
CHUNK = 2048
HALF = CHUNK // 2
SLOTS = 3
PIECE = 128
CUTS = 4
PIECES = 2
PHASES = 4
LEAD = 4
EARLY = 1
LATE = 2
PAIR = 1
BACK = 1


def dot(left_m, right_m, left_dim, right_dim, precision=None):
    return lax.dot_general(
        left_m,
        right_m,
        (((left_dim,), (right_dim,)), ((), ())),
        precision=precision,
        preferred_element_type=F32,
    )


def dot_full(left_m, right_m, left_dim, right_dim):
    return dot(left_m, right_m, left_dim, right_dim, lax.Precision.HIGHEST)


def split(value):
    high = value.astype(BF16)
    low = (value - high.astype(F32)).astype(BF16)
    return high, low


def inverse_factor(gram):
    k = gram.shape[0]
    line = lax.broadcasted_iota(jnp.int32, (k, k), 0)
    lane = lax.broadcasted_iota(jnp.int32, (k, k), 1)
    wide_line = lax.broadcasted_iota(jnp.int32, (k, 2 * k), 0)
    ident = jnp.where(line == lane, 1.0, 0.0).astype(F32)
    table = jnp.concatenate([gram, ident], axis=1)
    for j in range(0, k, 2):
        column0 = jnp.broadcast_to(table[:, j : j + 1], (k, 2 * k))
        column1 = jnp.broadcast_to(table[:, j + 1 : j + 2], (k, 2 * k))
        pivot0 = column0[j : j + 1]
        under = column0[j + 1 : j + 2]
        beside = column1[j : j + 1] / pivot0
        pivot1 = column1[j + 1 : j + 2] - under * beside
        row0 = table[j : j + 1] / pivot0
        row1 = (table[j + 1 : j + 2] - under * row0) / pivot1
        column1 = jnp.where(wide_line > j + 1, column1 - column0 * beside, 0.0)
        column0 = jnp.where(wide_line > j, column0, 0.0)
        table = table - column0 * row0 - column1 * row1
    diag = jnp.sum(jnp.where(line == lane, table[:, :k], 0.0), axis=1, keepdims=True)
    return table[:, k:] / jnp.sqrt(diag)


def below(gram, f11):
    h = f11.shape[0]
    l21 = dot_full(gram[:, 0:h], f11, 1, 1)
    return l21, gram[:, h : 2 * h] - dot_full(l21, l21, 1, 1)


def kernel(
    ranks, batch_total, scale,
    stress, sketch, basis_out, coeffs_out, spectrum_out,
    stage, high, low, operand, part, got1, summed, got2, panel,
    acc, gacc, spread, landed, total, full, zone, lead, basis, held, sums, spectrum, spect, gram, grams, lead_factor,
    stage_sem, small_sem, basis_sem, send1, recv1, send2, recv2, send3, recv3,
    rs_send, rs_recv, ag_send, ag_recv, sp_send, sp_recv, gr_send, gr_recv,
):
    groups = 4
    k = sketch.shape[0]
    kp = k // 2
    width = stress.shape[1]
    chunks = summed.shape[0]
    lines = kp // ranks
    me_row = lax.axis_index("rows")
    me = lax.axis_index("snaps")
    mine = me % 2
    core = me + 1 - 2 * mine
    chip = (me + 2) % groups
    units = PHASES * chunks
    per = chunks // groups
    blocks = [(i, h, (2 * i + h) * HALF) for i in range(per) for h in range(2)]

    def load(c, q):
        slot = c % SLOTS
        rows = CHUNK // CUTS
        return pltpu.make_async_copy(
            stress.at[pl.ds(c * CHUNK + q * rows, rows), :],
            stage.at[slot, pl.ds(q * rows, rows), :],
            stage_sem.at[slot, q],
        )

    sketch_copy = pltpu.make_async_copy(sketch, held, small_sem.at[0])
    coeffs_copy = pltpu.make_async_copy(sums, coeffs_out, small_sem.at[1])
    spectrum_copy = pltpu.make_async_copy(spectrum, spectrum_out, small_sem.at[2])
    load(0, 0).start()
    sketch_copy.start()
    for q in range(1, CUTS):
        load(0, q).start()

    barrier = pltpu.get_barrier_semaphore()
    for d in range(1, ranks):
        pl.semaphore_signal(
            barrier, inc=1, device_id={"rows": (me_row + d) % ranks}, device_id_type=MESH
        )
    for d in range(1, groups):
        pl.semaphore_signal(
            barrier, inc=1, device_id={"snaps": (me + d) % groups}, device_id_type=MESH
        )

    def remote(src, dst, s_sem, r_sem, device):
        return pltpu.make_async_remote_copy(
            src_ref=src, dst_ref=dst, send_sem=s_sem, recv_sem=r_sem,
            device_id=device, device_id_type=MESH,
        )

    def hop1(p, c):
        return remote(
            part.at[c, 1 - mine], got1.at[p, c], send1.at[p, c], recv1.at[p, c],
            {"snaps": core},
        )

    def hop2(p, c):
        return remote(summed.at[c], got2.at[p, c], send2.at[p, c], recv2.at[p, c], {"snaps": chip})

    def hop3(p, c):
        return remote(
            panel.at[p, c, mine], panel.at[p, c, mine], send3.at[p, c], recv3.at[p, c],
            {"snaps": core},
        )

    def scatter(p, d, lanes=None):
        to = (me_row + d) % ranks
        src, dst = spread.at[p, to], landed.at[p, d]
        if lanes is not None:
            src, dst = src.at[:, 0:lanes], dst.at[:, 0:lanes]
        return remote(src, dst, rs_send.at[p, d], rs_recv.at[p, d], {"rows": to})

    def gather(p, d, lanes=None):
        to = (me_row + d) % ranks
        src, dst = total.at[p], full.at[p, me_row]
        if lanes is not None:
            src, dst = src.at[:, 0:lanes], dst.at[:, 0:lanes]
        return remote(src, dst, ag_send.at[p, d], ag_recv.at[p, d], {"rows": to})

    def give_gram(d):
        return remote(
            gram, grams.at[me_row], gr_send.at[d], gr_recv.at[d], {"rows": (me_row + d) % ranks}
        )

    def share_spectrum(d):
        return remote(
            spect.at[0], spect.at[d], sp_send.at[d], sp_recv.at[d], {"snaps": (me + d) % groups}
        )

    def basis_copy(i):
        at = pl.ds(i * kp, kp)
        return pltpu.make_async_copy(basis.at[at, :], basis_out.at[at, :], basis_sem.at[i])

    def convert(c):
        slot = c % SLOTS

        @pl.when(c + 1 < chunks)
        def _():
            for q in range(CUTS):
                load(c + 1, q).start()

        per_cut = CHUNK // CUTS // PIECE
        for q in range(CUTS):
            load(c, q).wait()

            def body(i, carry):
                h, l = split(stage[slot, pl.ds(i * PIECE, PIECE), :])
                at = pl.ds(c * CHUNK + i * PIECE, PIECE)
                high[at, :] = h
                low[at, :] = l
                return carry

            lax.fori_loop(q * per_cut, (q + 1) * per_cut, body, 0, unroll=True)

    def project(p, c, h):
        at = pl.ds(c * CHUNK + h * HALF, HALF)
        both = dot(operand[p], high[at, :], 1, 1)
        rest = dot(operand[p, 0:kp, :], low[at, :], 1, 1)
        part[c, h] = both[0:kp] + (both[kp:k] + rest)

    def produce(p, c):
        @pl.when(p == 0)
        def _():
            convert(c)

        project(p, c, 1 - mine)

        @pl.when(jnp.logical_and(p == 0, c == 0))
        def _():
            pl.semaphore_wait(barrier, ranks - 1 + groups - 1)

        hop1(p, c).start()
        project(p, c, mine)

    def add_cores(p, c):
        hop1(p, c).wait()
        summed[c] = part[c, mine] + got1[p, c]
        hop2(p, c).start()

    def add_chips(p, c):
        hop2(p, c).wait()
        panel[p, c, mine] = summed[c] + got2[p, c]
        hop3(p, c).start()

    def stacked(p, c, h):
        hi, lo = split(panel[p, c, h])
        return jnp.concatenate([hi, lo], axis=0)

    def accumulate(p, c, h):
        stack = stacked(p, c, h)
        at = pl.ds(c * CHUNK + h * HALF, HALF)
        both = dot(stack, high[at, :], 1, 0)
        rest = dot(stack[0:kp], low[at, :], 1, 0)
        acc[:, 0:width] += both[0:kp] + (both[kp:k] + rest)

        @pl.when(p % 2 == 0)
        def _():
            gacc[:, 0:k] += dot(stack, stack, 1, 1)

        @pl.when(p % 2 == 1)
        def _():
            gacc[...] += dot(stack, jnp.concatenate([stacked(p - 1, c, h), stack], axis=0), 1, 1)

    def fold_gram():
        rows = gacc[0:kp, :] + gacc[kp:k, :]
        for i in range(2):
            at = i * k
            acc[:, width + i * kp : width + (i + 1) * kp] = (
                rows[:, at : at + kp] + rows[:, at + kp : at + k]
            )
        gacc[...] = jnp.zeros_like(gacc)

    def reduce_start(p, lanes=None):
        for r in range(ranks):
            spread[p, r] = acc[r * lines : (r + 1) * lines, :]
        acc[...] = jnp.zeros_like(acc)
        for d in range(1, ranks):
            scatter(p, d, lanes).start()

    def reduce_share(p, lanes=None):
        value = spread[p, me_row]
        for d in range(1, ranks):
            scatter(p, d, lanes).wait()
            value = value + landed[p, d]
        total[p] = value
        full[p, me_row] = value
        for d in range(1, ranks):
            gather(p, d, lanes).start()

    def reduce_end(p, lanes=None):
        for d in range(1, ranks):
            gather(p, d, lanes).wait()
        for r in range(ranks):
            zone[r * lines : (r + 1) * lines, :] = full[p, r]

    def set_operand(p, value):
        h, l = split(value)
        operand[p, 0:kp, :] = h
        operand[p, kp:k, :] = l

    acc[...] = jnp.zeros_like(acc)
    gacc[...] = jnp.zeros_like(gacc)
    sketch_copy.wait()
    for i in range(2):
        set_operand(i, held[i * kp : (i + 1) * kp, :])

    def step(s, carry):
        @pl.when(s < units)
        def _():
            produce(s // chunks, s % chunks)

        @pl.when(jnp.logical_and(s >= PAIR, s < units + PAIR))
        def _():
            u = s - PAIR
            add_cores(u // chunks, u % chunks)

        @pl.when(jnp.logical_and(s >= PAIR + LEAD, s < units + PAIR + LEAD))
        def _():
            u = s - PAIR - LEAD
            add_chips(u // chunks, u % chunks)

        @pl.when(s >= PAIR + LEAD + BACK)
        def _():
            u = s - PAIR - LEAD - BACK
            p, c = u // chunks, u % chunks
            hop3(p, c).wait()
            accumulate(p, c, 1 - mine)

        since = s - (chunks - 1 + PAIR + LEAD + BACK)
        done = since // chunks
        at = since % chunks
        live = jnp.logical_and(since >= 0, done < PHASES - 1)

        @pl.when(jnp.logical_and(live, at == 0))
        def _():
            fold_gram()
            reduce_start(done)

        @pl.when(jnp.logical_and(live, at == EARLY))
        def _():
            reduce_share(done)

        @pl.when(jnp.logical_and(live, at == LATE))
        def _():
            reduce_end(done)

            @pl.when(done % 2 == 0)
            def _():
                f11 = inverse_factor(zone[:, width : width + kp])
                value = dot_full(f11, zone[:, 0:width], 1, 0)
                lead_factor[...] = f11
                lead[...] = value
                set_operand(2, value)

            @pl.when(done == 1)
            def _():
                l21, rest = below(zone[:, width : width + k], lead_factor[...])
                f22 = inverse_factor(rest)
                value = zone[:, 0:width] - dot_full(l21, lead[...], 1, 0)
                set_operand(3, dot_full(f22, value, 1, 0))

            @pl.when(done == 2)
            def _():
                scaled = lead_factor[...] * scale
                for i, h, at in blocks:
                    value = panel[2, me * per + i, h]
                    basis[0:kp, at : at + HALF] = dot_full(scaled, value, 1, 0)
                basis_copy(0).start()

        @pl.when(jnp.logical_and(s >= PAIR + LEAD, s < units + PAIR + LEAD))
        def _():
            u = s - PAIR - LEAD
            accumulate(u // chunks, u % chunks, mine)

        return carry

    lax.fori_loop(0, units + PAIR + LEAD + BACK, step, 0)

    reduce_start(3, width)
    fold_gram()
    own_gram = acc[:, width : width + k]
    gram[...] = own_gram
    grams[me_row] = own_gram
    for d in range(1, ranks):
        give_gram(d).start()
    reduce_share(3, width)
    for d in range(1, ranks):
        give_gram(d).wait_recv()
    gram_total = grams[0]
    for r in range(1, ranks):
        gram_total = gram_total + grams[r]
    l21, rest = below(gram_total, lead_factor[...])
    top = lead[...]
    f22 = inverse_factor(rest)
    low_top = dot_full(l21, top, 1, 0)
    reduce_end(3, width)
    found = jnp.concatenate([top, dot_full(f22, zone[:, 0:width] - low_top, 1, 0)], axis=0)
    sums[...] = found
    stack = jnp.concatenate(split(found), axis=0)
    both = dot(stack, stack, 1, 1)
    rows = both[0:k] + both[k : 2 * k]
    spect[0] = rows[:, 0:k] + rows[:, k : 2 * k]
    for d in range(1, groups):
        share_spectrum(d).start()
    coeffs_copy.start()
    for i, h, at in blocks:
        value = panel[3, me * per + i, h]
        basis[kp:k, at : at + HALF] = scale * value - dot_full(l21, basis[0:kp, at : at + HALF], 1, 0)
    for i, h, at in blocks:
        basis[kp:k, at : at + HALF] = dot_full(f22, basis[kp:k, at : at + HALF], 1, 0)
    basis_copy(1).start()
    for d in range(1, ranks):
        give_gram(d).wait_send()
    for d in range(1, groups):
        share_spectrum(d).wait()
    a = spect[0] + spect[2]
    b = spect[1] + spect[3]
    spectrum[...] = (a + b) / batch_total
    spectrum_copy.start()
    coeffs_copy.wait()
    for i in range(2):
        basis_copy(i).wait()
    spectrum_copy.wait()


def finish(basis, coeffs, spectrum, basis_out, coeffs_out, spectrum_out, hold, rows, tiny, came, went):
    lines = basis.shape[0] // PIECES
    routes = [(coeffs, rows, coeffs_out), (spectrum, tiny, spectrum_out)]
    for i in range(PIECES):
        at = pl.ds(i * lines, lines)
        routes.append((basis.at[at, :], hold.at[at, :], basis_out.at[at, :]))
    loads = [pltpu.make_async_copy(r[0], r[1], came.at[i]) for i, r in enumerate(routes)]
    stores = [pltpu.make_async_copy(r[1], r[2], went.at[i]) for i, r in enumerate(routes)]
    for load in loads:
        load.start()
    for load, store in zip(loads, stores):
        load.wait()
        store.start()
    for store in stores:
        store.wait()


def on_device(stress, sketch):
    rows_dev, width = stress.shape
    k = sketch.shape[0]
    kp = k // 2
    groups = lax.axis_size("snaps")
    ranks = lax.axis_size("rows")
    share = rows_dev // groups
    chunks = rows_dev // CHUNK
    lines = kp // ranks
    wide = width + 128
    scale = math.sqrt(float(rows_dev * ranks))
    anywhere = pl.BlockSpec(memory_space=pl.ANY)
    dma = pltpu.SemaphoreType.DMA
    found = pl.pallas_call(
        functools.partial(kernel, ranks, float(width * groups), scale),
        out_shape=(
            jax.ShapeDtypeStruct((k, share), F32),
            jax.ShapeDtypeStruct((k, width), F32),
            jax.ShapeDtypeStruct((k, k), F32),
        ),
        in_specs=[anywhere] * 2,
        out_specs=(anywhere,) * 3,
        scratch_shapes=[
            pltpu.VMEM((SLOTS, CHUNK, width), F32),
            pltpu.VMEM((rows_dev, width), BF16),
            pltpu.VMEM((rows_dev, width), BF16),
            pltpu.VMEM((PHASES, k, width), BF16),
            pltpu.VMEM((chunks, 2, kp, HALF), F32),
            pltpu.VMEM((PHASES, chunks, kp, HALF), F32),
            pltpu.VMEM((chunks, kp, HALF), F32),
            pltpu.VMEM((PHASES, chunks, kp, HALF), F32),
            pltpu.VMEM((PHASES, chunks, 2, kp, HALF), F32),
            pltpu.VMEM((kp, wide), F32),
            pltpu.VMEM((k, 2 * k), F32),
            pltpu.VMEM((PHASES, ranks, lines, wide), F32),
            pltpu.VMEM((PHASES, ranks, lines, wide), F32),
            pltpu.VMEM((PHASES, lines, wide), F32),
            pltpu.VMEM((PHASES, ranks, lines, wide), F32),
            pltpu.VMEM((kp, wide), F32),
            pltpu.VMEM((kp, width), F32),
            pltpu.VMEM((k, share), F32),
            pltpu.VMEM((k, width), F32),
            pltpu.VMEM((k, width), F32),
            pltpu.VMEM((k, k), F32),
            pltpu.VMEM((groups, k, k), F32),
            pltpu.VMEM((kp, k), F32),
            pltpu.VMEM((ranks, kp, k), F32),
            pltpu.VMEM((kp, kp), F32),
            dma((SLOTS, CUTS)),
            dma((3,)),
            dma((2,)),
            dma((PHASES, chunks)),
            dma((PHASES, chunks)),
            dma((PHASES, chunks)),
            dma((PHASES, chunks)),
            dma((PHASES, chunks)),
            dma((PHASES, chunks)),
            dma((PHASES, ranks)),
            dma((PHASES, ranks)),
            dma((PHASES, ranks)),
            dma((PHASES, ranks)),
            dma((groups,)),
            dma((groups,)),
            dma((ranks,)),
            dma((ranks,)),
        ],
        compiler_params=pltpu.CompilerParams(
            collective_id=0, has_side_effects=True, vmem_limit_bytes=58 * 1024 * 1024
        ),
        cost_estimate=pl.CostEstimate(
            flops=24 * rows_dev * width * k, bytes_accessed=rows_dev * width * 4, transcendentals=0
        ),
    )(stress, sketch)
    return pl.pallas_call(
        finish,
        out_shape=tuple(jax.ShapeDtypeStruct(a.shape, a.dtype) for a in found),
        in_specs=[anywhere] * 3,
        out_specs=(anywhere,) * 3,
        scratch_shapes=[
            pltpu.VMEM((k, share), F32),
            pltpu.VMEM((k, width), F32),
            pltpu.VMEM((k, k), F32),
            dma((PIECES + 2,)),
            dma((PIECES + 2,)),
        ],
    )(*found)


def solution(mesh):
    placed = (P("rows", "snaps"), P(None, "snaps"))
    return jax.shard_map(
        on_device,
        mesh=mesh,
        in_specs=placed,
        out_specs=(P(None, ("rows", "snaps")), P(None, "snaps"), P()),
        check_vma=False,
    )
```
